256 devices in a mesh: tm: 8 (over y, core), space: 8 (over x, z_lo), clip: 4 (over z_hi).
Axes of the slice: x: 4, y: 4, z: 8 (z_hi: 4, z_lo: 2; z = z_hi * 2 + z_lo), core: 2. Of those that a mesh axis runs over, the one named last changes fastest.
Arguments:
- video: bfloat16 [16, 16, 1024, 512], P('clip', 'tm', 'space'), may hold values from -6 to 6
- conv_weight: bfloat16 [3, 512, 512], replicated, may hold values from -0.25 to 0.25
- norm_gain: float32 [512], replicated, may hold values from 0.1 to 1.9
- qkv_weight: bfloat16 [512, 1536], replicated
- out_weight: bfloat16 [512, 512], replicated, may hold values from -0.25 to 0.25
- cotangent: bfloat16 [16, 16, 1024, 512], P('clip', 'tm', 'space'), may hold values from -6 to 6
- lengths: int32 [16], P('clip'), may hold values from 5 to 16, as said below
Outputs:
- block_out: bfloat16 [16, 16, 1024, 512], P('clip', 'tm', 'space')
- out_weight_grad: float32 [512, 512], replicated
The draws below stay inside these ranges and needn't reach their ends.
Inputs may be any that keep to these rules, and one draw needn't show every extreme that they name: `lengths`: some clip has exactly 16 valid frames in every draw.
All inputs are finite; a program needn't handle non-finite values.
Results may differ from the reference program's by a relative error of at most 0.017.
Values may be sent and summed in bfloat16 or wider, within the bound.
No kernel may reach another device: no remote copies, remote signals or barrier semaphores. Data moves between devices by JAX's collectives and lax.ppermute only.
A program may use at most 64 MiB of HBM per device.

```python
import jax
import jax.numpy as jnp
from jax import lax

D = 512
CLIPS = 16
FRAMES = 16
PIX = 1024


def draw_qkv_weight(key, part):
    key = jax.random.fold_in(key, 11)
    scale = D ** (-0.5)
    base = jax.random.normal(key, (D, 3 * D), jnp.float32) * scale
    return base.astype(jnp.bfloat16)


def draw_lengths(key, part):
    key = jax.random.fold_in(key, 23)
    spread = jax.random.randint(key, (CLIPS,), FRAMES // 4 + 1, FRAMES + 1)
    chosen = jax.random.randint(jax.random.fold_in(key, 7), (), 0, CLIPS)
    return jnp.where(jnp.arange(CLIPS) == chosen, FRAMES, spread).astype(jnp.int32)


def level_of(stream_key, shape, shards, low, top_value):
    level, own = 1.0, jax.random.fold_in(stream_key, 6)
    for dim, blocks in shards:
        steps = jnp.exp(jax.random.uniform(jax.random.fold_in(own, dim), (blocks,), jnp.float32, low / len(shards), top_value / len(shards)))
        level = level * jnp.repeat(steps, shape[dim] // blocks).reshape([-1 if axis == dim else 1 for axis in range(len(shape))])
    return level


def normal_values(key, extent, scale, reach, cuts=(), held_as=jnp.bfloat16):
    result = scale * jax.random.normal(key, extent, jnp.float32)
    if cuts:
        result = result * level_of(key, extent, cuts, -0.22, 0.18)
    return jnp.clip(result, -reach, reach).astype(held_as)


def setup_inputs(seed: int = 0) -> dict:
    seeds = jax.random.split(jax.random.key(seed), 8)
    return {
        "video": normal_values(seeds[0], (CLIPS, FRAMES, PIX, D), 1.0, 6.0, ((0, 4), (1, 8), (2, 8))),
        "conv_weight": normal_values(seeds[1], (3, D, D), D ** -0.5, 0.25),
        "norm_gain": jnp.clip(1.0 + 0.18 * jax.random.normal(seeds[2], (D,), jnp.float32), 0.1, 1.9),
        "qkv_weight": draw_qkv_weight(jax.random.fold_in(seeds[7], 71), 0),
        "out_weight": normal_values(seeds[4], (D, D), D ** -0.5, 0.25),
        "cotangent": normal_values(seeds[5], (CLIPS, FRAMES, PIX, D), 1.0, 6.0, ((0, 4), (1, 8), (2, 8))),
        "lengths": draw_lengths(jax.random.fold_in(seeds[7], 71), 0),
    }


def attend_frame(frame):
    query_rows, key_rows, value_rows = frame
    scores = jnp.dot(query_rows, key_rows.T, preferred_element_type=jnp.float32) / jnp.sqrt(jnp.float32(query_rows.shape[-1]))
    top = lax.optimization_barrier(jnp.max(scores, axis=-1, keepdims=True))
    expo = jnp.exp(scores - top)
    weights = (expo / lax.optimization_barrier(jnp.sum(expo, axis=-1, keepdims=True))).astype(jnp.bfloat16)
    return jnp.dot(weights, value_rows, preferred_element_type=jnp.float32).astype(jnp.bfloat16)

def reference(video, conv_weight, norm_gain, qkv_weight, out_weight, cotangent, lengths):
    channels = video.shape[-1]
    padded = jnp.concatenate([jnp.zeros((CLIPS, 2, PIX, channels), jnp.bfloat16), video], axis=1)
    conv_sum = jnp.zeros((CLIPS * FRAMES * PIX, channels), jnp.float32)
    for offset in range(3):
        window = padded[:, 2 - offset:2 - offset + FRAMES].reshape(-1, channels)
        conv_sum = conv_sum + jnp.dot(window, conv_weight[offset], preferred_element_type=jnp.float32)
    hidden = (video.reshape(-1, channels).astype(jnp.float32) + conv_sum).astype(jnp.bfloat16)
    wide = hidden.astype(jnp.float32)
    normed = (wide * lax.rsqrt(lax.optimization_barrier(jnp.mean(wide * wide, axis=-1, keepdims=True)) + 1e-06) * norm_gain).astype(jnp.bfloat16)
    projected = jnp.dot(normed, qkv_weight, preferred_element_type=jnp.float32).astype(jnp.bfloat16)
    projected = projected.reshape(CLIPS * FRAMES, PIX, 3 * channels)
    attended = lax.map(attend_frame, (projected[..., :channels], projected[..., channels:2 * channels], projected[..., 2 * channels:]))
    attended_rows = attended.reshape(-1, channels)
    block_out = (hidden.astype(jnp.float32) + jnp.dot(attended_rows, out_weight, preferred_element_type=jnp.float32)).astype(jnp.bfloat16)
    frame_index = jnp.arange(FRAMES, dtype=jnp.int32)
    live_mask = (frame_index[None, :] < lengths[:, None]).astype(jnp.bfloat16)
    masked = (cotangent * live_mask[:, :, None, None]).reshape(-1, channels)
    out_weight_grad = lax.dot_general(attended_rows, masked, (((0,), (0,)), ((), ())), preferred_element_type=jnp.float32)
    return (block_out.reshape(video.shape), out_weight_grad)
```

```python
import functools

import jax
import jax.numpy as jnp
from jax import lax
from jax.experimental import pallas as pl
from jax.experimental.pallas import tpu as pltpu
from jax.sharding import Mesh, PartitionSpec as P

BF, F32 = jnp.bfloat16, jnp.float32
TIME = ("y", "core")
TILE = ("x", "zl")


def swap(x, axis, other):
    return lax.all_to_all(x, axis, split_axis=0, concat_axis=0, tiled=True)


def a2a(x, axes):
    return lax.all_to_all(x, axes, split_axis=0, concat_axis=0, tiled=True)


def group_size(axes):
    size = 1
    for axis in axes:
        size *= lax.axis_size(axis)
    return size


def conv_kernel(video_ref, early_ref, weight_ref, out_ref):
    half = video_ref.shape[2]

    def dot(rows, tap):
        return jnp.dot(rows, weight_ref[tap], preferred_element_type=F32)

    for clip in range(video_ref.shape[0]):
        v0, v1 = video_ref[clip, 0], video_ref[clip, 1]
        e0, e1 = early_ref[clip, 0], early_ref[clip, 1]
        out_ref[clip, 0] = (
            v0.astype(F32) + (dot(v0, 0) + dot(e1, 1) + dot(e0, 2))
        ).astype(BF)
        out_ref[clip, 1] = (
            v1.astype(F32) + (dot(v1, 0) + dot(v0, 1) + dot(e1, 2))
        ).astype(BF)


def attend_kernel(live_ref, hidden_ref, cot_ref, gain_ref, qkv_ref, wo_ref, out_ref, grad_ref, q_s, k_s, v_s):
    pixels, channels = hidden_ref.shape
    step = 256
    for i in range(pixels // step):
        rows = pl.ds(i * step, step)
        wide = hidden_ref[rows, :].astype(F32)
        mean = jnp.mean(wide * wide, axis=-1, keepdims=True)
        normed = (wide * lax.rsqrt(mean + 1e-06) * gain_ref[...]).astype(BF)
        for j, dst in enumerate((q_s, k_s, v_s)):
            dst[rows, :] = jnp.dot(
                normed, qkv_ref[:, j * channels : (j + 1) * channels], preferred_element_type=F32
            ).astype(BF)
    scale = 1.4426950408889634 / channels**0.5
    grad = jnp.zeros((channels, channels), F32)
    for i in range(pixels // step):
        rows = pl.ds(i * step, step)
        scores = lax.dot_general(
            q_s[rows, :], k_s[...], (((1,), (1,)), ((), ())), preferred_element_type=F32
        )
        top = jnp.max(scores, axis=-1, keepdims=True)
        expo = jnp.exp2((scores - top) * scale)
        total = jnp.sum(expo, axis=-1, keepdims=True)
        attended = (
            jnp.dot(expo.astype(BF), v_s[...], preferred_element_type=F32) / total
        ).astype(BF)
        out_ref[rows, :] = (
            hidden_ref[rows, :].astype(F32)
            + jnp.dot(attended, wo_ref[...], preferred_element_type=F32)
        ).astype(BF)
        grad = grad + lax.dot_general(
            attended, cot_ref[rows, :], (((0,), (0,)), ((), ())), preferred_element_type=F32
        )
    grad_ref[...] = grad * live_ref[0]


def scattered_sum(x, axes):
    n = group_size(axes)
    parts = a2a(x.astype(BF).reshape(n, x.shape[0] // n, x.shape[1]), axes)
    return jnp.sum(parts.astype(F32), axis=0)


def gathered(x, axes):
    n = group_size(axes)
    return a2a(jnp.broadcast_to(x[None], (n,) + x.shape), axes).reshape(n * x.shape[0], x.shape[1])


def exchanged(x, axis, by):
    n = lax.axis_size(axis)
    return lax.ppermute(x, axis, [(i, i ^ by) for i in range(n)])


def total_sum(grad):
    rows = grad.shape[0] // 2
    core = lax.axis_index("core")
    mine = lax.dynamic_slice_in_dim(grad, core * rows, rows, 0)
    other = lax.dynamic_slice_in_dim(grad, (1 - core) * rows, rows, 0).astype(BF)
    x = mine + exchanged(other, "core", 1).astype(F32)
    x = scattered_sum(x, ("y",) + TILE)
    for by in (1, 2):
        x = x + exchanged(x.astype(BF), "clip", by).astype(F32)
    x = gathered(x.astype(BF), ("y",) + TILE)
    other = exchanged(x, "core", 1)
    first = jnp.where(core == 0, x, other)
    second = jnp.where(core == 0, other, x)
    return jnp.concatenate([first, second], 0).astype(F32)


def body(video, conv_weight, norm_gain, qkv_weight, out_weight, cotangent, lengths):
    clips, frames, tile, channels = video.shape
    peers = clips * frames
    slabs = lax.axis_size(TIME)
    early = lax.ppermute(video, TIME, [(i, i + 1) for i in range(slabs - 1)])
    cot = a2a(cotangent.reshape(peers, tile, channels), TILE).reshape(peers * tile, channels)
    vmem = pl.BlockSpec(memory_space=pltpu.VMEM)
    params = pltpu.CompilerParams(vmem_limit_bytes=48 * 1024 * 1024)
    hidden = pl.pallas_call(
        conv_kernel,
        out_shape=jax.ShapeDtypeStruct(video.shape, BF),
        in_specs=[vmem] * 3,
        out_specs=vmem,
        compiler_params=params,
        name="conv",
    )(video, early, conv_weight)
    frame = a2a(hidden.reshape(peers, tile, channels), TILE).reshape(peers * tile, channels)
    place = lax.axis_index(TILE)
    moment = lax.axis_index(TIME) * frames + place % frames
    live = (moment < lengths[place // frames]).astype(F32).reshape(1)
    out, grad = pl.pallas_call(
        attend_kernel,
        out_shape=(
            jax.ShapeDtypeStruct(frame.shape, BF),
            jax.ShapeDtypeStruct((channels, channels), F32),
        ),
        in_specs=[pl.BlockSpec(memory_space=pltpu.SMEM)] + [vmem] * 5,
        out_specs=(vmem, vmem),
        scratch_shapes=[pltpu.VMEM(frame.shape, BF)] * 3,
        compiler_params=params,
        name="attend",
    )(live, frame, cot, norm_gain.reshape(1, channels), qkv_weight, out_weight)
    block_out = a2a(out.reshape(peers, tile, channels), TILE).reshape(video.shape)
    return block_out, total_sum(grad)


def solution(mesh):
    fine = Mesh(mesh.devices.reshape(4, 2, 4, 2, 4), ("y", "core", "x", "zl", "clip"))
    part = P("clip", TIME, TILE, None)
    in_specs = (part, P(), P(), P(), P(), part, P("clip"))
    return jax.shard_map(body, mesh=fine, in_specs=in_specs, out_specs=(part, P()), check_vma=False)
```

```python
import jax
import jax.numpy as jnp
from jax import lax
from jax.experimental import pallas as pl
from jax.experimental.pallas import tpu as pltpu
from jax.sharding import Mesh, PartitionSpec as P

BF, F32 = jnp.bfloat16, jnp.float32
TIME = ("y", "core")
TILE = ("x", "zl")
PLANE = ("y", "x")
DEPTH = ("zl", "clip")
ANY = pl.BlockSpec(memory_space=pl.ANY)
VMEM = pl.BlockSpec(memory_space=pltpu.VMEM)
SMEM = pl.BlockSpec(memory_space=pltpu.SMEM)
PARAMS = pltpu.CompilerParams(vmem_limit_bytes=12 * 1024 * 1024)


def a2a(x, axes):
    return lax.all_to_all(x, axes, split_axis=0, concat_axis=0, tiled=True)


def group_size(axes):
    size = 1
    for axis in axes:
        size *= lax.axis_size(axis)
    return size


def call(kernel, name, out_shape, in_specs, out_specs, *args, **more):
    return pl.pallas_call(
        kernel,
        out_shape=out_shape,
        in_specs=in_specs,
        out_specs=out_specs,
        compiler_params=PARAMS,
        name=name,
        **more,
    )(*args)


def after(x, *others):
    def kernel(*refs):
        pass

    return call(
        kernel,
        "after",
        jax.ShapeDtypeStruct(x.shape, x.dtype),
        [ANY] * (1 + len(others)),
        ANY,
        x,
        *others,
        input_output_aliases={0: 0},
    )


def own_kernel(video_ref, weight_ref, own_ref):
    def dot(rows, tap):
        return jnp.dot(rows, weight_ref[tap], preferred_element_type=F32)

    rows = (own_ref.shape[0] * own_ref.shape[2], own_ref.shape[3])
    v0, v1 = video_ref[:, 0].reshape(rows), video_ref[:, 1].reshape(rows)
    own_ref[:, 0] = (v0.astype(F32) + dot(v0, 0)).reshape(own_ref[:, 0].shape)
    own_ref[:, 1] = (v1.astype(F32) + (dot(v1, 0) + dot(v0, 1))).reshape(own_ref[:, 0].shape)


def early_kernel(own_ref, early_ref, weight_ref, out_ref):
    def dot(rows, tap):
        return jnp.dot(rows, weight_ref[tap], preferred_element_type=F32)

    rows = (own_ref.shape[0] * own_ref.shape[2], own_ref.shape[3])
    e0, e1 = early_ref[:, 0].reshape(rows), early_ref[:, 1].reshape(rows)
    h0 = own_ref[:, 0].reshape(rows) + (dot(e1, 1) + dot(e0, 2))
    h1 = own_ref[:, 1].reshape(rows) + dot(e1, 2)
    out_ref[:, 0] = h0.astype(BF).reshape(out_ref[:, 0].shape)
    out_ref[:, 1] = h1.astype(BF).reshape(out_ref[:, 1].shape)


def attend_kernel(
    hidden_ref, gain_ref, qkv_ref, att_ref, q_s, k_s, v_s
):
    pixels, channels = att_ref.shape
    step = 256
    steps = pixels // step

    def chunk(i):
        return pl.ds(i * step, step)

    def normed(i):
        wide = hidden_ref[chunk(i), :].astype(F32)
        mean = jnp.mean(wide * wide, axis=-1, keepdims=True)
        return (wide * lax.rsqrt(mean + 1e-06) * gain_ref[...]).astype(BF)

    ready = normed(0)
    for i in range(steps):
        following = normed(i + 1) if i + 1 < steps else None
        for j, dst in enumerate((q_s, k_s, v_s)):
            dst[chunk(i), :] = jnp.dot(
                ready, qkv_ref[:, j * channels : (j + 1) * channels], preferred_element_type=F32
            ).astype(BF)
        ready = following
    scale = 1.4426950408889634 / channels**0.5

    def scored(i):
        return lax.dot_general(
            q_s[chunk(i), :], k_s[...], (((1,), (1,)), ((), ())), preferred_element_type=F32
        )

    def weighed(scores):
        top = jnp.max(scores, axis=-1, keepdims=True)
        expo = jnp.exp2((scores - top) * scale)
        return expo.astype(BF), jnp.sum(expo, axis=-1, keepdims=True)

    def attended(expo, total):
        mixed = jnp.dot(expo, v_s[...], preferred_element_type=F32)
        return (mixed * (1.0 / total)).astype(BF)

    stages = [{} for _ in range(2)]
    for t in range(steps + 2):
        if t < steps:
            stages[0][t] = scored(t)
        if 0 <= t - 1 < steps:
            stages[1][t - 1] = weighed(stages[0].pop(t - 1))
        if 0 <= t - 2 < steps:
            att_ref[chunk(t - 2), :] = attended(*stages[1].pop(t - 2))


def grad_kernel(place_ref, lengths_ref, att_ref, cot_ref, mine_ref, other_ref, cot_s, g_s):
    clips, frames, tile, channels = cot_ref.shape
    for clip in range(clips):
        for frame in range(frames):
            live = place_ref[0] * frames + frame < lengths_ref[clip]
            rows = pl.ds((clip * frames + frame) * tile, tile)
            cot_s[rows, :] = cot_ref[clip, frame] * jnp.where(live, 1.0, 0.0).astype(BF)
    g_s[...] = lax.dot_general(
        att_ref[...], cot_s[...], (((0,), (0,)), ((), ())), preferred_element_type=F32
    )
    core = place_ref[1]
    split = channels // 2
    mine_ref[...] = g_s[pl.ds(pl.multiple_of(core * split, split), split), :]
    other_ref[...] = g_s[pl.ds(pl.multiple_of((1 - core) * split, split), split), :].astype(BF)


def out_kernel(hidden_ref, att_ref, wo_ref, out_ref):
    out_ref[...] = (
        hidden_ref[...].astype(F32)
        + jnp.dot(att_ref[...], wo_ref[...], preferred_element_type=F32)
    ).astype(BF)


def exchanged(x, axis, by):
    n = lax.axis_size(axis)
    return lax.ppermute(x, axis, [(i, i ^ by) for i in range(n)])


def spread(x, axes):
    n = group_size(axes)
    return a2a(jnp.broadcast_to(x.astype(BF)[None], (n,) + x.shape), axes)


def total_sum(mine, other):
    core = lax.axis_index("core")
    x = mine + exchanged(other, "core", 1).astype(F32)
    n = group_size(PLANE)
    x = a2a(x.astype(BF).reshape(n, x.shape[0] // n, x.shape[1]), PLANE)
    x = jnp.sum(x.astype(F32), axis=0)
    x = jnp.sum(spread(x, DEPTH).astype(F32), axis=0).astype(BF)
    x = spread(x, PLANE).reshape(mine.shape)
    other = exchanged(x, "core", 1)
    first = jnp.where(core == 0, x, other)
    second = jnp.where(core == 0, other, x)
    return jnp.concatenate([first, second], 0).astype(F32)


def body(video, conv_weight, norm_gain, qkv_weight, out_weight, cotangent, lengths):
    clips, frames, tile, channels = video.shape
    peers = clips * frames
    slabs = lax.axis_size(TIME)
    early = lax.ppermute(video, TIME, [(i, i + 1) for i in range(slabs - 1)])
    own = call(
        own_kernel,
        "own",
        jax.ShapeDtypeStruct(video.shape, F32),
        [VMEM] * 2,
        VMEM,
        video, conv_weight,
    )
    hidden = call(
        early_kernel,
        "early",
        jax.ShapeDtypeStruct(video.shape, BF),
        [VMEM] * 3,
        VMEM,
        own, early, conv_weight,
        cost_estimate=pl.CostEstimate(flops=30_000_000_000, bytes_accessed=1 << 22, transcendentals=0),
    )
    rows = jax.ShapeDtypeStruct((peers * tile, channels), BF)
    frame = a2a(hidden.reshape(peers, tile, channels), TILE).reshape(rows.shape)
    att = call(
        attend_kernel,
        "attend",
        rows,
        [VMEM] * 3,
        VMEM,
        frame, norm_gain.reshape(1, channels), qkv_weight,
        scratch_shapes=[pltpu.VMEM(rows.shape, BF)] * 3,
    )
    att = a2a(att.reshape(peers, tile, channels), TILE).reshape(rows.shape)
    places = jnp.stack([lax.axis_index(TIME), lax.axis_index("core")])
    split = jax.ShapeDtypeStruct((channels // 2, channels), F32)
    mine, other = call(
        grad_kernel,
        "grad",
        (split, jax.ShapeDtypeStruct(split.shape, BF)),
        [SMEM, SMEM, VMEM, VMEM],
        (VMEM, VMEM),
        places, lengths, att, cotangent,
        scratch_shapes=[pltpu.VMEM(rows.shape, BF), pltpu.VMEM((channels, channels), F32)],
    )
    out = call(
        out_kernel,
        "out",
        rows,
        [VMEM] * 3,
        VMEM,
        hidden.reshape(rows.shape), att, out_weight,
    )
    return out.reshape(video.shape), total_sum(mine, other)


def solution(mesh):
    fine = Mesh(mesh.devices.reshape(4, 2, 4, 2, 4), ("y", "core", "x", "zl", "clip"))
    part = P("clip", TIME, TILE, None)
    in_specs = (part, P(), P(), P(), P(), part, P("clip"))
    return jax.shard_map(body, mesh=fine, in_specs=in_specs, out_specs=(part, P()), check_vma=False)
```

```python
import jax
import jax.numpy as jnp
from jax import lax
from jax.experimental import pallas as pl
from jax.experimental.pallas import tpu as pltpu
from jax.sharding import Mesh, PartitionSpec as P

BF, F32 = jnp.bfloat16, jnp.float32
TIME = ("y", "core")
TILE = ("x", "zl")
PLANE = ("y", "x")
DEPTH = ("zl", "clip")
ANY = pl.BlockSpec(memory_space=pl.ANY)
VMEM = pl.BlockSpec(memory_space=pltpu.VMEM)
SMEM = pl.BlockSpec(memory_space=pltpu.SMEM)
PARAMS = pltpu.CompilerParams(vmem_limit_bytes=12 * 1024 * 1024)


def a2a(x, axes):
    return lax.all_to_all(x, axes, split_axis=0, concat_axis=0, tiled=True)


def group_size(axes):
    size = 1
    for axis in axes:
        size *= lax.axis_size(axis)
    return size


def call(kernel, name, out_shape, in_specs, out_specs, *args, **more):
    return pl.pallas_call(
        kernel,
        out_shape=out_shape,
        in_specs=in_specs,
        out_specs=out_specs,
        compiler_params=PARAMS,
        name=name,
        **more,
    )(*args)


def after(x, *others):
    def kernel(*refs):
        pass

    return call(
        kernel,
        "after",
        jax.ShapeDtypeStruct(x.shape, x.dtype),
        [ANY] * (1 + len(others)),
        ANY,
        x,
        *others,
        input_output_aliases={0: 0},
    )


def own_kernel(video_ref, weight_ref, own_ref):
    def dot(rows, tap):
        return jnp.dot(rows, weight_ref[tap], preferred_element_type=F32)

    rows = (own_ref.shape[0] * own_ref.shape[2], own_ref.shape[3])
    v0, v1 = video_ref[:, 0].reshape(rows), video_ref[:, 1].reshape(rows)
    own_ref[:, 0] = (v0.astype(F32) + dot(v0, 0)).reshape(own_ref[:, 0].shape)
    own_ref[:, 1] = (v1.astype(F32) + (dot(v1, 0) + dot(v0, 1))).reshape(own_ref[:, 0].shape)


def early_kernel(own_ref, first_ref, second_ref, weight_ref, out_ref):
    half = first_ref.shape[0]
    shape = (half,) + own_ref.shape[2:]
    rows = (shape[0] * shape[1], shape[2])

    def dot(rows, tap):
        return jnp.dot(rows, weight_ref[tap], preferred_element_type=F32)

    for i, early_ref in enumerate((first_ref, second_ref)):
        at = pl.ds(i * half, half)
        e0, e1 = early_ref[:, 0].reshape(rows), early_ref[:, 1].reshape(rows)
        h0 = own_ref[at, 0].reshape(rows) + (dot(e1, 1) + dot(e0, 2))
        h1 = own_ref[at, 1].reshape(rows) + dot(e1, 2)
        out_ref[at, 0] = h0.astype(BF).reshape(shape)
        out_ref[at, 1] = h1.astype(BF).reshape(shape)


def attend_kernel(
    hidden_ref, gain_ref, qkv_ref, att_ref, q_s, k_s, v_s
):
    pixels, channels = att_ref.shape
    step = 256
    steps = pixels // step

    def chunk(i):
        return pl.ds(i * step, step)

    def normed(i):
        wide = hidden_ref[chunk(i), :].astype(F32)
        mean = jnp.mean(wide * wide, axis=-1, keepdims=True)
        return (wide * lax.rsqrt(mean + 1e-06) * gain_ref[...]).astype(BF)

    ready = normed(0)
    for i in range(steps):
        following = normed(i + 1) if i + 1 < steps else None
        for j, dst in enumerate((q_s, k_s, v_s)):
            dst[chunk(i), :] = jnp.dot(
                ready, qkv_ref[:, j * channels : (j + 1) * channels], preferred_element_type=F32
            ).astype(BF)
        ready = following
    scale = 1.4426950408889634 / channels**0.5

    def scored(i):
        return lax.dot_general(
            q_s[chunk(i), :], k_s[...], (((1,), (1,)), ((), ())), preferred_element_type=F32
        )

    def weighed(scores):
        top = jnp.max(scores, axis=-1, keepdims=True)
        expo = jnp.exp2((scores - top) * scale)
        return expo.astype(BF), jnp.sum(expo, axis=-1, keepdims=True)

    def attended(expo, total):
        mixed = jnp.dot(expo, v_s[...], preferred_element_type=F32)
        return (mixed * (1.0 / total)).astype(BF)

    stages = [{} for _ in range(2)]
    for t in range(steps + 2):
        if t < steps:
            stages[0][t] = scored(t)
        if 0 <= t - 1 < steps:
            stages[1][t - 1] = weighed(stages[0].pop(t - 1))
        if 0 <= t - 2 < steps:
            att_ref[chunk(t - 2), :] = attended(*stages[1].pop(t - 2))


def grad_kernel(place_ref, lengths_ref, att_ref, cot_ref, mine_ref, other_ref, cot_s, g_s):
    clips, frames, tile, channels = cot_ref.shape
    for clip in range(clips):
        for frame in range(frames):
            live = place_ref[0] * frames + frame < lengths_ref[clip]
            rows = pl.ds((clip * frames + frame) * tile, tile)
            cot_s[rows, :] = cot_ref[clip, frame] * jnp.where(live, 1.0, 0.0).astype(BF)
    g_s[...] = lax.dot_general(
        att_ref[...], cot_s[...], (((0,), (0,)), ((), ())), preferred_element_type=F32
    )
    core = place_ref[1]
    split = channels // 2
    mine_ref[...] = g_s[pl.ds(pl.multiple_of(core * split, split), split), :]
    other_ref[...] = g_s[pl.ds(pl.multiple_of((1 - core) * split, split), split), :].astype(BF)


def out_kernel(hidden_ref, att_ref, wo_ref, out_ref):
    out_ref[...] = (
        hidden_ref[...].astype(F32)
        + jnp.dot(att_ref[...], wo_ref[...], preferred_element_type=F32)
    ).astype(BF)


def exchanged(x, axis, by):
    n = lax.axis_size(axis)
    return lax.ppermute(x, axis, [(i, i ^ by) for i in range(n)])


def spread(x, axes):
    n = group_size(axes)
    return a2a(jnp.broadcast_to(x.astype(BF)[None], (n,) + x.shape), axes)


def total_sum(mine, other):
    core = lax.axis_index("core")
    x = mine + exchanged(other, "core", 1).astype(F32)
    n = group_size(PLANE)
    x = a2a(x.astype(BF).reshape(n, x.shape[0] // n, x.shape[1]), PLANE)
    x = jnp.sum(x.astype(F32), axis=0)
    x = jnp.sum(spread(x, DEPTH).astype(F32), axis=0).astype(BF)
    x = spread(x, PLANE).reshape(mine.shape)
    other = exchanged(x, "core", 1)
    first = jnp.where(core == 0, x, other)
    second = jnp.where(core == 0, other, x)
    return jnp.concatenate([first, second], 0).astype(F32)


def body(video, conv_weight, norm_gain, qkv_weight, out_weight, cotangent, lengths):
    clips, frames, tile, channels = video.shape
    peers = clips * frames
    slabs = lax.axis_size(TIME)
    half = clips // 2
    early = [lax.ppermute(video[:half], TIME, [(i, i + 1) for i in range(slabs - 1)])]
    near = exchanged(video, "core", 1)[half:]
    ahead = [(i, i + 2) for i in range(0, slabs - 2, 2)]
    early.append(lax.ppermute(near, TIME, ahead + [(i, i) for i in range(1, slabs, 2)]))
    own = call(
        own_kernel,
        "own",
        jax.ShapeDtypeStruct(video.shape, F32),
        [VMEM] * 2,
        VMEM,
        video, conv_weight,
    )
    hidden = call(
        early_kernel,
        "early",
        jax.ShapeDtypeStruct(video.shape, BF),
        [VMEM] * 4,
        VMEM,
        own, *early, conv_weight,
        cost_estimate=pl.CostEstimate(flops=30_000_000_000, bytes_accessed=1 << 22, transcendentals=0),
    )
    rows = jax.ShapeDtypeStruct((peers * tile, channels), BF)
    frame = a2a(hidden.reshape(peers, tile, channels), TILE).reshape(rows.shape)
    att = call(
        attend_kernel,
        "attend",
        rows,
        [VMEM] * 3,
        VMEM,
        frame, norm_gain.reshape(1, channels), qkv_weight,
        scratch_shapes=[pltpu.VMEM(rows.shape, BF)] * 3,
    )
    att = a2a(att.reshape(peers, tile, channels), TILE).reshape(rows.shape)
    places = jnp.stack([lax.axis_index(TIME), lax.axis_index("core")])
    split = jax.ShapeDtypeStruct((channels // 2, channels), F32)
    mine, other = call(
        grad_kernel,
        "grad",
        (split, jax.ShapeDtypeStruct(split.shape, BF)),
        [SMEM, SMEM, VMEM, VMEM],
        (VMEM, VMEM),
        places, lengths, att, cotangent,
        scratch_shapes=[pltpu.VMEM(rows.shape, BF), pltpu.VMEM((channels, channels), F32)],
    )
    out = call(
        out_kernel,
        "out",
        rows,
        [VMEM] * 3,
        VMEM,
        hidden.reshape(rows.shape), att, out_weight,
    )
    return out.reshape(video.shape), total_sum(mine, other)


def solution(mesh):
    fine = Mesh(mesh.devices.reshape(4, 2, 4, 2, 4), ("y", "core", "x", "zl", "clip"))
    part = P("clip", TIME, TILE, None)
    in_specs = (part, P(), P(), P(), P(), part, P("clip"))
    return jax.shard_map(body, mesh=fine, in_specs=in_specs, out_specs=(part, P()), check_vma=False)
```

```python
import jax
import jax.numpy as jnp
from jax import lax
from jax.experimental import pallas as pl
from jax.experimental.pallas import tpu as pltpu
from jax.sharding import Mesh, PartitionSpec as P

BF, F32 = jnp.bfloat16, jnp.float32
TIME = ("y", "core")
TILE = ("x", "zl")
PLANE = ("y", "x")
DEPTH = ("zl", "clip")
ANY = pl.BlockSpec(memory_space=pl.ANY)
VMEM = pl.BlockSpec(memory_space=pltpu.VMEM)
SMEM = pl.BlockSpec(memory_space=pltpu.SMEM)
PARAMS = pltpu.CompilerParams(vmem_limit_bytes=12 * 1024 * 1024)


def a2a(x, axes):
    return lax.all_to_all(x, axes, split_axis=0, concat_axis=0, tiled=True)


def group_size(axes):
    size = 1
    for axis in axes:
        size *= lax.axis_size(axis)
    return size


def call(kernel, name, out_shape, in_specs, out_specs, *args, **more):
    return pl.pallas_call(
        kernel,
        out_shape=out_shape,
        in_specs=in_specs,
        out_specs=out_specs,
        compiler_params=PARAMS,
        name=name,
        **more,
    )(*args)


def after(x, *others):
    def kernel(*refs):
        pass

    return call(
        kernel,
        "after",
        jax.ShapeDtypeStruct(x.shape, x.dtype),
        [ANY] * (1 + len(others)),
        ANY,
        x,
        *others,
        input_output_aliases={0: 0},
    )


def own_kernel(place_ref, video_ref, weight_ref, qkv_ref, own_ref, pair_ref, value_ref):
    channels = video_ref.shape[-1]
    pair_ref[...] = lax.dot_general(
        qkv_ref[:, :channels],
        qkv_ref[:, channels : 2 * channels],
        (((1,), (1,)), ((), ())),
        preferred_element_type=F32,
    ).astype(BF)
    value_ref[...] = qkv_ref[:, 2 * channels :]

    def dot(rows, tap):
        return jnp.dot(rows, weight_ref[tap], preferred_element_type=F32)

    rows = (own_ref.shape[0] * own_ref.shape[2], own_ref.shape[3])
    v0, v1 = video_ref[:, 0].reshape(rows), video_ref[:, 1].reshape(rows)
    own_ref[:, 0] = (v0.astype(F32) + dot(v0, 0)).reshape(own_ref[:, 0].shape)
    own_ref[:, 1] = (v1.astype(F32) + (dot(v1, 0) + dot(v0, 1))).reshape(own_ref[:, 0].shape)


def early_kernel(own_ref, first_ref, second_ref, weight_ref, out_ref):
    half = first_ref.shape[0]
    shape = (half,) + own_ref.shape[2:]
    rows = (shape[0] * shape[1], shape[2])

    def dot(rows, tap):
        return jnp.dot(rows, weight_ref[tap], preferred_element_type=F32)

    for i, early_ref in enumerate((first_ref, second_ref)):
        at = pl.ds(i * half, half)
        e0, e1 = early_ref[:, 0].reshape(rows), early_ref[:, 1].reshape(rows)
        h0 = own_ref[at, 0].reshape(rows) + (dot(e1, 1) + dot(e0, 2))
        h1 = own_ref[at, 1].reshape(rows) + dot(e1, 2)
        out_ref[at, 0] = h0.astype(BF).reshape(shape)
        out_ref[at, 1] = h1.astype(BF).reshape(shape)


def attend_kernel(
    hidden_ref, gain_ref, pair_ref, value_ref, att_ref, q_s, k_s, v_s
):
    pixels, channels = att_ref.shape
    step = 256
    steps = pixels // step

    def chunk(i):
        return pl.ds(i * step, step)

    def normed(i):
        wide = hidden_ref[chunk(i), :].astype(F32)
        mean = jnp.mean(wide * wide, axis=-1, keepdims=True)
        return (wide * lax.rsqrt(mean + 1e-06) * gain_ref[...]).astype(BF)

    ready = normed(0)
    for i in range(steps):
        following = normed(i + 1) if i + 1 < steps else None
        q_s[chunk(i), :] = jnp.dot(ready, pair_ref[...], preferred_element_type=F32).astype(BF)
        k_s[chunk(i), :] = ready
        v_s[chunk(i), :] = jnp.dot(ready, value_ref[...], preferred_element_type=F32).astype(BF)
        ready = following
    scale = 1.4426950408889634 / channels**0.5

    def scored(i):
        return lax.dot_general(
            q_s[chunk(i), :], k_s[...], (((1,), (1,)), ((), ())), preferred_element_type=F32
        )

    def weighed(scores):
        top = jnp.max(scores, axis=-1, keepdims=True)
        expo = jnp.exp2((scores - top) * scale)
        return expo.astype(BF), jnp.sum(expo, axis=-1, keepdims=True)

    def attended(expo, total):
        mixed = jnp.dot(expo, v_s[...], preferred_element_type=F32)
        return (mixed * (1.0 / total)).astype(BF)

    stages = [{} for _ in range(2)]
    for t in range(steps + 2):
        if t < steps:
            stages[0][t] = scored(t)
        if 0 <= t - 1 < steps:
            stages[1][t - 1] = weighed(stages[0].pop(t - 1))
        if 0 <= t - 2 < steps:
            att_ref[chunk(t - 2), :] = attended(*stages[1].pop(t - 2))


def grad_kernel(place_ref, lengths_ref, att_ref, cot_ref, mine_ref, other_ref, cot_s, g_s):
    clips, frames, tile, channels = cot_ref.shape
    for clip in range(clips):
        for frame in range(frames):
            live = place_ref[0] * frames + frame < lengths_ref[clip]
            rows = pl.ds((clip * frames + frame) * tile, tile)
            cot_s[rows, :] = cot_ref[clip, frame] * jnp.where(live, 1.0, 0.0).astype(BF)
    g_s[...] = lax.dot_general(
        att_ref[...], cot_s[...], (((0,), (0,)), ((), ())), preferred_element_type=F32
    )
    core = place_ref[1]
    split = channels // 2
    mine_ref[...] = g_s[pl.ds(pl.multiple_of(core * split, split), split), :]
    other_ref[...] = g_s[pl.ds(pl.multiple_of((1 - core) * split, split), split), :].astype(BF)


def out_kernel(hidden_ref, att_ref, wo_ref, out_ref):
    out_ref[...] = (
        hidden_ref[...].astype(F32)
        + jnp.dot(att_ref[...], wo_ref[...], preferred_element_type=F32)
    ).astype(BF)


def exchanged(x, axis, by):
    n = lax.axis_size(axis)
    return lax.ppermute(x, axis, [(i, i ^ by) for i in range(n)])


def spread(x, axes):
    n = group_size(axes)
    return a2a(jnp.broadcast_to(x.astype(BF)[None], (n,) + x.shape), axes)


def total_sum(mine, other):
    core = lax.axis_index("core")
    x = mine + exchanged(other, "core", 1).astype(F32)
    n = group_size(PLANE)
    x = a2a(x.astype(BF).reshape(n, x.shape[0] // n, x.shape[1]), PLANE)
    x = jnp.sum(x.astype(F32), axis=0)
    x = jnp.sum(spread(x, DEPTH).astype(F32), axis=0).astype(BF)
    x = spread(x, PLANE).reshape(mine.shape)
    other = exchanged(x, "core", 1)
    first = jnp.where(core == 0, x, other)
    second = jnp.where(core == 0, other, x)
    return jnp.concatenate([first, second], 0).astype(F32)


def body(video, conv_weight, norm_gain, qkv_weight, out_weight, cotangent, lengths):
    clips, frames, tile, channels = video.shape
    peers = clips * frames
    slabs = lax.axis_size(TIME)
    half = clips // 2
    early = [lax.ppermute(video[:half], TIME, [(i, i + 1) for i in range(slabs - 1)])]
    near = exchanged(video, "core", 1)[half:]
    ahead = [(i, i + 2) for i in range(0, slabs - 2, 2)]
    early.append(lax.ppermute(near, TIME, ahead + [(i, i) for i in range(1, slabs, 2)]))
    places = jnp.stack([lax.axis_index(TIME), lax.axis_index("core")])
    own, pair, value = call(
        own_kernel,
        "own",
        (jax.ShapeDtypeStruct(video.shape, F32),) + (jax.ShapeDtypeStruct(out_weight.shape, BF),) * 2,
        [SMEM] + [VMEM] * 3,
        (VMEM,) * 3,
        places, video, conv_weight, qkv_weight,
    )
    hidden = call(
        early_kernel,
        "early",
        jax.ShapeDtypeStruct(video.shape, BF),
        [VMEM] * 4,
        VMEM,
        own, *early, conv_weight,
        cost_estimate=pl.CostEstimate(flops=30_000_000_000, bytes_accessed=1 << 22, transcendentals=0),
    )
    rows = jax.ShapeDtypeStruct((peers * tile, channels), BF)
    frame = a2a(hidden.reshape(peers, tile, channels), TILE).reshape(rows.shape)
    att = call(
        attend_kernel,
        "attend",
        rows,
        [VMEM] * 4,
        VMEM,
        frame, norm_gain.reshape(1, channels), pair, value,
        scratch_shapes=[pltpu.VMEM(rows.shape, BF)] * 3,
    )
    att = a2a(att.reshape(peers, tile, channels), TILE).reshape(rows.shape)
    split = jax.ShapeDtypeStruct((channels // 2, channels), F32)
    mine, other = call(
        grad_kernel,
        "grad",
        (split, jax.ShapeDtypeStruct(split.shape, BF)),
        [SMEM, SMEM, VMEM, VMEM],
        (VMEM, VMEM),
        places, lengths, att, cotangent,
        scratch_shapes=[pltpu.VMEM(rows.shape, BF), pltpu.VMEM((channels, channels), F32)],
    )
    out = call(
        out_kernel,
        "out",
        rows,
        [VMEM] * 3,
        VMEM,
        hidden.reshape(rows.shape), att, out_weight,
    )
    return out.reshape(video.shape), total_sum(mine, other)


def solution(mesh):
    fine = Mesh(mesh.devices.reshape(4, 2, 4, 2, 4), ("y", "core", "x", "zl", "clip"))
    part = P("clip", TIME, TILE, None)
    in_specs = (part, P(), P(), P(), P(), part, P("clip"))
    return jax.shard_map(body, mesh=fine, in_specs=in_specs, out_specs=(part, P()), check_vma=False)
```

```python
import functools

import jax
import jax.numpy as jnp
from jax import lax
from jax.experimental import pallas as pl
from jax.experimental.pallas import tpu as pltpu
from jax.sharding import Mesh, PartitionSpec as P

BF, F32 = jnp.bfloat16, jnp.float32
TIME = ("y", "core")
TILE = ("x", "zl")
PLANE = ("y", "x")
DEPTH = ("zl", "clip")
ANY = pl.BlockSpec(memory_space=pl.ANY)
VMEM = pl.BlockSpec(memory_space=pltpu.VMEM)
SMEM = pl.BlockSpec(memory_space=pltpu.SMEM)
PARAMS = pltpu.CompilerParams(vmem_limit_bytes=12 * 1024 * 1024)


def a2a(x, axes):
    return lax.all_to_all(x, axes, split_axis=0, concat_axis=0, tiled=True)


def group_size(axes):
    size = 1
    for axis in axes:
        size *= lax.axis_size(axis)
    return size


def call(kernel, name, out_shape, in_specs, out_specs, *args, **more):
    return pl.pallas_call(
        kernel,
        out_shape=out_shape,
        in_specs=in_specs,
        out_specs=out_specs,
        compiler_params=PARAMS,
        name=name,
        **more,
    )(*args)


def after(x, *others):
    def kernel(*refs):
        pass

    return call(
        kernel,
        "after",
        jax.ShapeDtypeStruct(x.shape, x.dtype),
        [ANY] * (1 + len(others)),
        ANY,
        x,
        *others,
        input_output_aliases={0: 0},
    )


def own_kernel(place_ref, video_ref, weight_ref, qkv_ref, own_ref, pair_ref, value_ref):
    channels = video_ref.shape[-1]
    pair_ref[...] = lax.dot_general(
        qkv_ref[:, :channels],
        qkv_ref[:, channels : 2 * channels],
        (((1,), (1,)), ((), ())),
        preferred_element_type=F32,
    ).astype(BF)
    value_ref[...] = qkv_ref[:, 2 * channels :]

    def dot(rows, tap):
        return jnp.dot(rows, weight_ref[tap], preferred_element_type=F32)

    rows = (own_ref.shape[0] * own_ref.shape[2], own_ref.shape[3])
    v0, v1 = video_ref[:, 0].reshape(rows), video_ref[:, 1].reshape(rows)
    own_ref[:, 0] = (v0.astype(F32) + dot(v0, 0)).reshape(own_ref[:, 0].shape)
    own_ref[:, 1] = (v1.astype(F32) + (dot(v1, 0) + dot(v0, 1))).reshape(own_ref[:, 0].shape)


def early_kernel(start, own_ref, early_ref, weight_ref, *refs):
    out_ref = refs[-1]
    shape = (early_ref.shape[0],) + early_ref.shape[2:]
    rows = (shape[0] * shape[1], shape[2])
    at = pl.ds(start, shape[0])

    def dot(rows, tap):
        return jnp.dot(rows, weight_ref[tap], preferred_element_type=F32)

    e0, e1 = early_ref[:, 0].reshape(rows), early_ref[:, 1].reshape(rows)
    h0 = own_ref[at, 0].reshape(rows) + (dot(e1, 1) + dot(e0, 2))
    h1 = own_ref[at, 1].reshape(rows) + dot(e1, 2)
    out_ref[at, 0] = h0.astype(BF).reshape(shape)
    out_ref[at, 1] = h1.astype(BF).reshape(shape)


def attend_kernel(
    hidden_ref, gain_ref, pair_ref, value_ref, att_ref, q_s, k_s, v_s
):
    pixels, channels = att_ref.shape
    step = 256
    steps = pixels // step

    def chunk(i):
        return pl.ds(i * step, step)

    def normed(i):
        wide = hidden_ref[chunk(i), :].astype(F32)
        mean = jnp.mean(wide * wide, axis=-1, keepdims=True)
        return (wide * lax.rsqrt(mean + 1e-06) * gain_ref[...]).astype(BF)

    ready = normed(0)
    for i in range(steps):
        following = normed(i + 1) if i + 1 < steps else None
        q_s[chunk(i), :] = jnp.dot(ready, pair_ref[...], preferred_element_type=F32).astype(BF)
        k_s[chunk(i), :] = ready
        v_s[chunk(i), :] = jnp.dot(ready, value_ref[...], preferred_element_type=F32).astype(BF)
        ready = following
    scale = 1.4426950408889634 / channels**0.5

    def scored(i):
        return lax.dot_general(
            q_s[chunk(i), :], k_s[...], (((1,), (1,)), ((), ())), preferred_element_type=F32
        )

    def weighed(scores):
        top = jnp.max(scores, axis=-1, keepdims=True)
        expo = jnp.exp2((scores - top) * scale)
        return expo.astype(BF), jnp.sum(expo, axis=-1, keepdims=True)

    def attended(expo, total):
        mixed = jnp.dot(expo, v_s[...], preferred_element_type=F32)
        return (mixed * (1.0 / total)).astype(BF)

    stages = [{} for _ in range(2)]
    for t in range(steps + 2):
        if t < steps:
            stages[0][t] = scored(t)
        if 0 <= t - 1 < steps:
            stages[1][t - 1] = weighed(stages[0].pop(t - 1))
        if 0 <= t - 2 < steps:
            att_ref[chunk(t - 2), :] = attended(*stages[1].pop(t - 2))


def grad_kernel(place_ref, lengths_ref, att_ref, cot_ref, grad_ref, live_ref, *, swap):
    clips, frames, tile = cot_ref.shape[:3]
    for clip in range(clips):
        for frame in range(frames):
            live = place_ref[0] * frames + frame < lengths_ref[clip]
            rows = pl.ds((clip * frames + frame) * tile, tile)
            live_ref[rows, :] = cot_ref[clip, frame] * jnp.where(live, 1.0, 0.0).astype(BF)
    split = grad_ref.shape[0]
    half = 1 - place_ref[1] if swap else place_ref[1]
    grad_ref[...] = lax.dot_general(
        att_ref[:, pl.ds(pl.multiple_of(half * split, split), split)],
        live_ref[...],
        (((0,), (0,)), ((), ())),
        preferred_element_type=F32,
    ).astype(grad_ref.dtype)


def out_kernel(hidden_ref, att_ref, wo_ref, out_ref):
    out_ref[...] = (
        hidden_ref[...].astype(F32)
        + jnp.dot(att_ref[...], wo_ref[...], preferred_element_type=F32)
    ).astype(BF)


def exchanged(x, axis, by):
    n = lax.axis_size(axis)
    return lax.ppermute(x, axis, [(i, i ^ by) for i in range(n)])


def spread(x, axes):
    n = group_size(axes)
    return a2a(jnp.broadcast_to(x.astype(BF)[None], (n,) + x.shape), axes)


def total_sum(mine, other):
    core = lax.axis_index("core")
    x = mine + exchanged(other, "core", 1).astype(F32)
    n = group_size(PLANE)
    x = a2a(x.astype(BF).reshape(n, x.shape[0] // n, x.shape[1]), PLANE)
    x = jnp.sum(x.astype(F32), axis=0)
    x = jnp.sum(spread(x, DEPTH).astype(F32), axis=0).astype(BF)
    x = spread(x, PLANE).reshape(mine.shape)
    other = exchanged(x, "core", 1)
    first = jnp.where(core == 0, x, other)
    second = jnp.where(core == 0, other, x)
    return jnp.concatenate([first, second], 0).astype(F32)


def body(video, conv_weight, norm_gain, qkv_weight, out_weight, cotangent, lengths):
    clips, frames, tile, channels = video.shape
    peers = clips * frames
    slabs = lax.axis_size(TIME)
    half = clips // 2
    early = [lax.ppermute(video[:half], TIME, [(i, i + 1) for i in range(slabs - 1)])]
    near = exchanged(video, "core", 1)[half:]
    ahead = [(i, i + 2) for i in range(0, slabs - 2, 2)]
    early.append(lax.ppermute(near, TIME, ahead + [(i, i) for i in range(1, slabs, 2)]))
    places = jnp.stack([lax.axis_index(TIME), lax.axis_index("core")])
    own, pair, value = call(
        own_kernel,
        "own",
        (jax.ShapeDtypeStruct(video.shape, F32),) + (jax.ShapeDtypeStruct(out_weight.shape, BF),) * 2,
        [SMEM] + [VMEM] * 3,
        (VMEM,) * 3,
        places, video, conv_weight, qkv_weight,
    )
    hidden = ()
    for i in range(2):
        hidden = call(
            functools.partial(early_kernel, i * half),
            "early%d" % i,
            jax.ShapeDtypeStruct(video.shape, BF),
            [VMEM] * (3 + i),
            VMEM,
            own, early[i], conv_weight, *hidden,
            input_output_aliases={3: 0} if i else {},
        )
        hidden = (hidden,)
    (hidden,) = hidden
    rows = jax.ShapeDtypeStruct((peers * tile, channels), BF)
    frame = a2a(hidden.reshape(peers, tile, channels), TILE).reshape(rows.shape)
    att = call(
        attend_kernel,
        "attend",
        rows,
        [VMEM] * 4,
        VMEM,
        frame, norm_gain.reshape(1, channels), pair, value,
        scratch_shapes=[pltpu.VMEM(rows.shape, BF)] * 3,
    )
    att = a2a(att.reshape(peers, tile, channels), TILE).reshape(rows.shape)
    other, mine = (
        call(
            functools.partial(grad_kernel, swap=swap),
            "other" if swap else "mine",
            jax.ShapeDtypeStruct((channels // 2, channels), BF if swap else F32),
            [SMEM, SMEM, VMEM, VMEM],
            VMEM,
            places, lengths, att, cotangent,
            scratch_shapes=[pltpu.VMEM(rows.shape, BF)],
            cost_estimate=pl.CostEstimate(flops=1 << 28, bytes_accessed=1 << 21, transcendentals=0),
        )
        for swap in (True, False)
    )
    out = call(
        out_kernel,
        "out",
        rows,
        [VMEM] * 3,
        VMEM,
        hidden.reshape(rows.shape), att, out_weight,
    )
    return out.reshape(video.shape), total_sum(mine, other)


def solution(mesh):
    fine = Mesh(mesh.devices.reshape(4, 2, 4, 2, 4), ("y", "core", "x", "zl", "clip"))
    part = P("clip", TIME, TILE, None)
    in_specs = (part, P(), P(), P(), P(), part, P("clip"))
    return jax.shard_map(body, mesh=fine, in_specs=in_specs, out_specs=(part, P()), check_vma=False)
```

```python
import functools

import jax
import jax.numpy as jnp
from jax import lax
from jax.experimental import pallas as pl
from jax.experimental.pallas import tpu as pltpu
from jax.sharding import Mesh, PartitionSpec as P

BF, F32 = jnp.bfloat16, jnp.float32
TIME = ("y", "core")
TILE = ("x", "zl")
PLANE = ("y", "x")
DEPTH = ("zl", "clip")
ANY = pl.BlockSpec(memory_space=pl.ANY)
VMEM = pl.BlockSpec(memory_space=pltpu.VMEM)
SMEM = pl.BlockSpec(memory_space=pltpu.SMEM)
PARAMS = pltpu.CompilerParams(vmem_limit_bytes=12 * 1024 * 1024)


def a2a(x, axes):
    return lax.all_to_all(x, axes, split_axis=0, concat_axis=0, tiled=True)


def group_size(axes):
    size = 1
    for axis in axes:
        size *= lax.axis_size(axis)
    return size


def call(kernel, name, out_shape, in_specs, out_specs, *args, **more):
    return pl.pallas_call(
        kernel,
        out_shape=out_shape,
        in_specs=in_specs,
        out_specs=out_specs,
        compiler_params=PARAMS,
        name=name,
        **more,
    )(*args)


def own_kernel(
    place_ref, video_ref, weight_ref, qkv_ref, cot_ref, own_ref, pair_ref, value_ref
):
    channels = video_ref.shape[-1]
    pair_ref[...] = lax.dot_general(
        qkv_ref[:, :channels],
        qkv_ref[:, channels : 2 * channels],
        (((1,), (1,)), ((), ())),
        preferred_element_type=F32,
    ).astype(BF)
    value_ref[...] = qkv_ref[:, 2 * channels :]

    def dot(rows, tap):
        return jnp.dot(rows, weight_ref[tap], preferred_element_type=F32)

    rows = (own_ref.shape[0] * own_ref.shape[2], own_ref.shape[3])
    v0, v1 = video_ref[:, 0].reshape(rows), video_ref[:, 1].reshape(rows)
    own_ref[:, 0] = (v0.astype(F32) + dot(v0, 0)).reshape(own_ref[:, 0].shape)
    own_ref[:, 1] = (v1.astype(F32) + (dot(v1, 0) + dot(v0, 1))).reshape(own_ref[:, 0].shape)


def early_kernel(own_ref, early_ref, weight_ref, out_ref):
    shape = (early_ref.shape[0],) + early_ref.shape[2:]
    rows = (shape[0] * shape[1], shape[2])

    def dot(rows, tap):
        return jnp.dot(rows, weight_ref[tap], preferred_element_type=F32)

    e0, e1 = early_ref[:, 0].reshape(rows), early_ref[:, 1].reshape(rows)
    h0 = own_ref[:, 0].reshape(rows) + (dot(e1, 1) + dot(e0, 2))
    h1 = own_ref[:, 1].reshape(rows) + dot(e1, 2)
    out_ref[:, 0] = h0.astype(BF).reshape(shape)
    out_ref[:, 1] = h1.astype(BF).reshape(shape)


def attend_kernel(
    hidden_ref, gain_ref, pair_ref, value_ref, att_ref, q_s, k_s, v_s
):
    pixels, channels = att_ref.shape
    step = 256
    steps = pixels // step

    def chunk(i):
        return pl.ds(i * step, step)

    def normed(i):
        wide = hidden_ref[chunk(i), :].astype(F32)
        mean = jnp.mean(wide * wide, axis=-1, keepdims=True)
        return (wide * lax.rsqrt(mean + 1e-06) * gain_ref[...]).astype(BF)

    ready = normed(0)
    for i in range(steps):
        following = normed(i + 1) if i + 1 < steps else None
        q_s[chunk(i), :] = jnp.dot(ready, pair_ref[...], preferred_element_type=F32).astype(BF)
        k_s[chunk(i), :] = ready
        v_s[chunk(i), :] = jnp.dot(ready, value_ref[...], preferred_element_type=F32).astype(BF)
        ready = following
    scale = 1.4426950408889634 / channels**0.5

    def scored(i):
        return lax.dot_general(
            q_s[chunk(i), :], k_s[...], (((1,), (1,)), ((), ())), preferred_element_type=F32
        )

    def weighed(scores):
        top = jnp.max(scores, axis=-1, keepdims=True)
        expo = jnp.exp2((scores - top) * scale)
        return expo.astype(BF), jnp.sum(expo, axis=-1, keepdims=True)

    def attended(expo, total):
        mixed = jnp.dot(expo, v_s[...], preferred_element_type=F32)
        return (mixed * (1.0 / total)).astype(BF)

    stages = [{} for _ in range(2)]
    for t in range(steps + 2):
        if t < steps:
            stages[0][t] = scored(t)
        if 0 <= t - 1 < steps:
            stages[1][t - 1] = weighed(stages[0].pop(t - 1))
        if 0 <= t - 2 < steps:
            att_ref[chunk(t - 2), :] = attended(*stages[1].pop(t - 2))


def grad_kernel(place_ref, lengths_ref, att_ref, cot_ref, grad_ref, live_ref, *, swap):
    clips, frames, tile = cot_ref.shape[:3]
    for clip in range(clips):
        for frame in range(frames):
            live = place_ref[0] * frames + frame < lengths_ref[clip]
            rows = pl.ds((clip * frames + frame) * tile, tile)
            live_ref[rows, :] = cot_ref[clip, frame] * jnp.where(live, 1.0, 0.0).astype(BF)
    split = grad_ref.shape[0]
    half = 1 - place_ref[1] if swap else place_ref[1]
    grad_ref[...] = lax.dot_general(
        att_ref[:, pl.ds(pl.multiple_of(half * split, split), split)],
        live_ref[...],
        (((0,), (0,)), ((), ())),
        preferred_element_type=F32,
    ).astype(grad_ref.dtype)


def out_kernel(hidden_ref, att_ref, wo_ref, out_ref):
    out_ref[...] = (
        hidden_ref[...].astype(F32)
        + jnp.dot(att_ref[...], wo_ref[...], preferred_element_type=F32)
    ).astype(BF)


def deliver_kernel(src_ref, out_ref, sems):
    each = src_ref.shape[0] // sems.shape[0]
    copies = [
        pltpu.make_async_copy(src_ref.at[pl.ds(i * each, each)], out_ref.at[pl.ds(i * each, each)], sems.at[i])
        for i in range(sems.shape[0])
    ]
    for copy in copies:
        copy.start()
    for copy in copies:
        copy.wait()


def exchanged(x, axis, by):
    n = lax.axis_size(axis)
    return lax.ppermute(x, axis, [(i, i ^ by) for i in range(n)])


def spread(x, axes):
    n = group_size(axes)
    return a2a(jnp.broadcast_to(x.astype(BF)[None], (n,) + x.shape), axes)


def total_sum(mine, other):
    core = lax.axis_index("core")
    x = mine + exchanged(other, "core", 1).astype(F32)
    n = group_size(PLANE)
    x = a2a(x.astype(BF).reshape(n, x.shape[0] // n, x.shape[1]), PLANE)
    x = jnp.sum(x.astype(F32), axis=0)
    x = jnp.sum(spread(x, DEPTH).astype(F32), axis=0).astype(BF)
    x = spread(x, PLANE).reshape(mine.shape)
    other = exchanged(x, "core", 1)
    first = jnp.where(core == 0, x, other)
    second = jnp.where(core == 0, other, x)
    return jnp.concatenate([first, second], 0).astype(F32)


def body(video, conv_weight, norm_gain, qkv_weight, out_weight, cotangent, lengths):
    clips, frames, tile, channels = video.shape
    peers = clips * frames
    slabs = lax.axis_size(TIME)
    onward = [(i, i + 2) for i in range(1, slabs - 2, 2)] + [(i, i) for i in range(0, slabs, 2)]
    early = lax.ppermute(video, TIME, onward)
    video = exchanged(video, "core", 1)
    cotangent = exchanged(cotangent, "core", 1)
    core = lax.axis_index("core")
    places = jnp.stack([lax.axis_index(TIME) + 1 - 2 * core, core])
    own, pair, value = call(
        own_kernel,
        "own",
        (jax.ShapeDtypeStruct(video.shape, F32),) + (jax.ShapeDtypeStruct(out_weight.shape, BF),) * 2,
        [SMEM] + [VMEM] * 3 + [ANY],
        (VMEM,) * 3,
        places, video, conv_weight, qkv_weight, cotangent,
    )
    hidden = call(
        early_kernel,
        "early",
        jax.ShapeDtypeStruct(video.shape, BF),
        [VMEM] * 3,
        VMEM,
        own, early, conv_weight,
    )
    rows = jax.ShapeDtypeStruct((peers * tile, channels), BF)
    frame = a2a(hidden.reshape(peers, tile, channels), TILE).reshape(rows.shape)
    att = call(
        attend_kernel,
        "attend",
        rows,
        [VMEM] * 4,
        VMEM,
        frame, norm_gain.reshape(1, channels), pair, value,
        scratch_shapes=[pltpu.VMEM(rows.shape, BF)] * 3,
    )
    att = a2a(att.reshape(peers, tile, channels), TILE).reshape(rows.shape)
    other, mine = (
        call(
            functools.partial(grad_kernel, swap=swap),
            "other" if swap else "mine",
            jax.ShapeDtypeStruct((channels // 2, channels), BF if swap else F32),
            [SMEM, SMEM, VMEM, VMEM],
            VMEM,
            places, lengths, att, cotangent,
            scratch_shapes=[pltpu.VMEM(rows.shape, BF)],
            cost_estimate=pl.CostEstimate(flops=1 << 28, bytes_accessed=1 << 21, transcendentals=0),
        )
        for swap in (True, False)
    )
    out = call(
        out_kernel,
        "out",
        rows,
        [VMEM] * 3,
        VMEM,
        hidden.reshape(rows.shape), att, out_weight,
    )
    out = call(
        deliver_kernel,
        "deliver",
        rows,
        [ANY],
        ANY,
        exchanged(out, "core", 1),
        scratch_shapes=[pltpu.SemaphoreType.DMA((peers,))],
        cost_estimate=pl.CostEstimate(flops=1 << 28, bytes_accessed=1 << 21, transcendentals=0),
    )
    return out.reshape(video.shape), total_sum(mine, other)


def solution(mesh):
    fine = Mesh(mesh.devices.reshape(4, 2, 4, 2, 4), ("y", "core", "x", "zl", "clip"))
    part = P("clip", TIME, TILE, None)
    in_specs = (part, P(), P(), P(), P(), part, P("clip"))
    return jax.shard_map(body, mesh=fine, in_specs=in_specs, out_specs=(part, P()), check_vma=False)
```

```python
import functools

import jax
import jax.numpy as jnp
from jax import lax
from jax.experimental import pallas as pl
from jax.experimental.pallas import tpu as pltpu
from jax.sharding import Mesh, PartitionSpec as P

BF, F32 = jnp.bfloat16, jnp.float32
TIME = ("y", "core")
TILE = ("x", "zl")
PLANE = ("y", "x")
DEPTH = ("zl", "clip")
ANY = pl.BlockSpec(memory_space=pl.ANY)
VMEM = pl.BlockSpec(memory_space=pltpu.VMEM)
SMEM = pl.BlockSpec(memory_space=pltpu.SMEM)
PARAMS = pltpu.CompilerParams(vmem_limit_bytes=12 * 1024 * 1024)


def a2a(x, axes):
    return lax.all_to_all(x, axes, split_axis=0, concat_axis=0, tiled=True)


def group_size(axes):
    size = 1
    for axis in axes:
        size *= lax.axis_size(axis)
    return size


def call(kernel, name, out_shape, in_specs, out_specs, *args, **more):
    return pl.pallas_call(
        kernel,
        out_shape=out_shape,
        in_specs=in_specs,
        out_specs=out_specs,
        compiler_params=PARAMS,
        name=name,
        **more,
    )(*args)


def own_kernel(
    place_ref, video_ref, weight_ref, qkv_ref, cot_ref, own_ref, pair_ref, value_ref
):
    channels = video_ref.shape[-1]
    pair_ref[...] = lax.dot_general(
        qkv_ref[:, :channels],
        qkv_ref[:, channels : 2 * channels],
        (((1,), (1,)), ((), ())),
        preferred_element_type=F32,
    ).astype(BF)
    value_ref[...] = qkv_ref[:, 2 * channels :]

    def dot(rows, tap):
        return jnp.dot(rows, weight_ref[tap], preferred_element_type=F32)

    rows = (own_ref.shape[0] * own_ref.shape[2], own_ref.shape[3])
    v0, v1 = video_ref[:, 0].reshape(rows), video_ref[:, 1].reshape(rows)
    own_ref[:, 0] = (v0.astype(F32) + dot(v0, 0)).reshape(own_ref[:, 0].shape)
    own_ref[:, 1] = (v1.astype(F32) + (dot(v1, 0) + dot(v0, 1))).reshape(own_ref[:, 0].shape)


def early_kernel(own_ref, early_ref, weight_ref, out_ref):
    shape = (early_ref.shape[0],) + early_ref.shape[2:]
    rows = (shape[0] * shape[1], shape[2])

    def dot(rows, tap):
        return jnp.dot(rows, weight_ref[tap], preferred_element_type=F32)

    e0, e1 = early_ref[:, 0].reshape(rows), early_ref[:, 1].reshape(rows)
    h0 = own_ref[:, 0].reshape(rows) + (dot(e1, 1) + dot(e0, 2))
    h1 = own_ref[:, 1].reshape(rows) + dot(e1, 2)
    out_ref[:, 0] = h0.astype(BF).reshape(shape)
    out_ref[:, 1] = h1.astype(BF).reshape(shape)


def attend_kernel(
    hidden_ref, gain_ref, pair_ref, value_ref, att_ref, q_s, k_s, v_s
):
    pixels, channels = att_ref.shape
    step = 256
    steps = pixels // step

    def chunk(i):
        return pl.ds(i * step, step)

    def normed(i):
        wide = hidden_ref[chunk(i), :].astype(F32)
        mean = jnp.mean(wide * wide, axis=-1, keepdims=True)
        return (wide * lax.rsqrt(mean + 1e-06) * gain_ref[...]).astype(BF)

    ready = normed(0)
    for i in range(steps):
        following = normed(i + 1) if i + 1 < steps else None
        q_s[chunk(i), :] = jnp.dot(ready, pair_ref[...], preferred_element_type=F32).astype(BF)
        k_s[chunk(i), :] = ready
        v_s[chunk(i), :] = jnp.dot(ready, value_ref[...], preferred_element_type=F32).astype(BF)
        ready = following
    scale = 1.4426950408889634 / channels**0.5

    def scored(i):
        return lax.dot_general(
            q_s[chunk(i), :], k_s[...], (((1,), (1,)), ((), ())), preferred_element_type=F32
        )

    def weighed(scores):
        top = jnp.max(scores, axis=-1, keepdims=True)
        expo = jnp.exp2((scores - top) * scale)
        return expo.astype(BF), jnp.sum(expo, axis=-1, keepdims=True)

    def attended(expo, total):
        mixed = jnp.dot(expo, v_s[...], preferred_element_type=F32)
        return (mixed * (1.0 / total)).astype(BF)

    stages = [{} for _ in range(2)]
    for t in range(steps + 2):
        if t < steps:
            stages[0][t] = scored(t)
        if 0 <= t - 1 < steps:
            stages[1][t - 1] = weighed(stages[0].pop(t - 1))
        if 0 <= t - 2 < steps:
            att_ref[chunk(t - 2), :] = attended(*stages[1].pop(t - 2))


def masked_into(live_ref, place_ref, lengths_ref, cot_ref):
    clips, frames, tile = cot_ref.shape[:3]
    for clip in range(clips):
        for frame in range(frames):
            live = place_ref[0] * frames + frame < lengths_ref[clip]
            rows = pl.ds((clip * frames + frame) * tile, tile)
            live_ref[rows, :] = cot_ref[clip, frame] * jnp.where(live, 1.0, 0.0).astype(BF)


def half_grad(att_ref, live_ref, half, split):
    return lax.dot_general(
        att_ref[:, pl.ds(pl.multiple_of(half * split, split), split)],
        live_ref[...],
        (((0,), (0,)), ((), ())),
        preferred_element_type=F32,
    )


def own_rows(hidden_ref, att_ref, wo_ref, out_ref):
    out_ref[...] = (
        hidden_ref[...].astype(F32)
        + jnp.dot(att_ref[...], wo_ref[...], preferred_element_type=F32)
    ).astype(BF)


def before_kernel(
    place_ref, lengths_ref, att_ref, cot_ref, hidden_ref, wo_ref,
    other_ref, live_ref, mine_ref, out_ref,
):
    masked_into(live_ref, place_ref, lengths_ref, cot_ref)
    split = other_ref.shape[0]
    other_ref[...] = half_grad(att_ref, live_ref, 1 - place_ref[1], split).astype(BF)

    @pl.when(place_ref[1] == 0)
    def _():
        mine_ref[...] = half_grad(att_ref, live_ref, 0, split)
        own_rows(hidden_ref, att_ref, wo_ref, out_ref)


def during_kernel(
    place_ref, att_ref, live_ref, hidden_ref, wo_ref, mine_in, out_in, mine_ref, out_ref
):
    @pl.when(place_ref[1] == 1)
    def _():
        own_rows(hidden_ref, att_ref, wo_ref, out_ref)
        mine_ref[...] = half_grad(att_ref, live_ref, 1, mine_ref.shape[0])

    @pl.when(place_ref[1] == 0)
    def _():
        mine_ref[...] = mine_in[...]
        out_ref[...] = out_in[...]


def deliver_kernel(src_ref, out_ref, sems):
    each = src_ref.shape[0] // sems.shape[0]
    copies = [
        pltpu.make_async_copy(src_ref.at[pl.ds(i * each, each)], out_ref.at[pl.ds(i * each, each)], sems.at[i])
        for i in range(sems.shape[0])
    ]
    for copy in copies:
        copy.start()
    for copy in copies:
        copy.wait()


def exchanged(x, axis, by):
    n = lax.axis_size(axis)
    return lax.ppermute(x, axis, [(i, i ^ by) for i in range(n)])


def spread(x, axes):
    n = group_size(axes)
    return a2a(jnp.broadcast_to(x.astype(BF)[None], (n,) + x.shape), axes)


def total_sum(mine, other):
    core = lax.axis_index("core")
    x = mine + exchanged(other, "core", 1).astype(F32)
    n = group_size(PLANE)
    x = a2a(x.astype(BF).reshape(n, x.shape[0] // n, x.shape[1]), PLANE)
    x = jnp.sum(x.astype(F32), axis=0)
    x = jnp.sum(spread(x, DEPTH).astype(F32), axis=0).astype(BF)
    x = spread(x, PLANE).reshape(mine.shape)
    other = exchanged(x, "core", 1)
    first = jnp.where(core == 0, x, other)
    second = jnp.where(core == 0, other, x)
    return jnp.concatenate([first, second], 0).astype(F32)


def body(video, conv_weight, norm_gain, qkv_weight, out_weight, cotangent, lengths):
    clips, frames, tile, channels = video.shape
    peers = clips * frames
    slabs = lax.axis_size(TIME)
    onward = [(i, i + 2) for i in range(1, slabs - 2, 2)] + [(i, i) for i in range(0, slabs, 2)]
    early = lax.ppermute(video, TIME, onward)
    video = exchanged(video, "core", 1)
    cotangent = exchanged(cotangent, "core", 1)
    core = lax.axis_index("core")
    places = jnp.stack([lax.axis_index(TIME) + 1 - 2 * core, core])
    own, pair, value = call(
        own_kernel,
        "own",
        (jax.ShapeDtypeStruct(video.shape, F32),) + (jax.ShapeDtypeStruct(out_weight.shape, BF),) * 2,
        [SMEM] + [VMEM] * 3 + [ANY],
        (VMEM,) * 3,
        places, video, conv_weight, qkv_weight, cotangent,
    )
    hidden = call(
        early_kernel,
        "early",
        jax.ShapeDtypeStruct(video.shape, BF),
        [VMEM] * 3,
        VMEM,
        own, early, conv_weight,
    )
    rows = jax.ShapeDtypeStruct((peers * tile, channels), BF)
    frame = a2a(hidden.reshape(peers, tile, channels), TILE).reshape(rows.shape)
    att = call(
        attend_kernel,
        "attend",
        rows,
        [VMEM] * 4,
        VMEM,
        frame, norm_gain.reshape(1, channels), pair, value,
        scratch_shapes=[pltpu.VMEM(rows.shape, BF)] * 3,
    )
    att = a2a(att.reshape(peers, tile, channels), TILE).reshape(rows.shape)
    kept = jax.ShapeDtypeStruct((channels // 2, channels), F32)
    flat = hidden.reshape(rows.shape)
    other, live, mine, out = call(
        before_kernel,
        "before",
        (jax.ShapeDtypeStruct(kept.shape, BF), rows, kept, rows),
        [SMEM] * 2 + [VMEM] * 4,
        (VMEM,) * 4,
        places, lengths, att, cotangent, flat, out_weight,
    )
    mine, out = call(
        during_kernel,
        "during",
        (kept, rows),
        [SMEM] + [VMEM] * 6,
        (VMEM,) * 2,
        places, att, live, flat, out_weight, mine, out,
        input_output_aliases={5: 0, 6: 1},
        cost_estimate=pl.CostEstimate(flops=1 << 29, bytes_accessed=1 << 21, transcendentals=0),
    )
    out = call(
        deliver_kernel,
        "deliver",
        rows,
        [ANY],
        ANY,
        exchanged(out, "core", 1),
        scratch_shapes=[pltpu.SemaphoreType.DMA((peers,))],
        cost_estimate=pl.CostEstimate(flops=1 << 28, bytes_accessed=1 << 21, transcendentals=0),
    )
    return out.reshape(video.shape), total_sum(mine, other)


def solution(mesh):
    fine = Mesh(mesh.devices.reshape(4, 2, 4, 2, 4), ("y", "core", "x", "zl", "clip"))
    part = P("clip", TIME, TILE, None)
    in_specs = (part, P(), P(), P(), P(), part, P("clip"))
    return jax.shard_map(body, mesh=fine, in_specs=in_specs, out_specs=(part, P()), check_vma=False)
```

```python
import functools

import jax
import jax.numpy as jnp
from jax import lax
from jax.experimental import pallas as pl
from jax.experimental.pallas import tpu as pltpu
from jax.sharding import Mesh, PartitionSpec as P

BF, F32 = jnp.bfloat16, jnp.float32
TIME = ("y", "core")
TILE = ("x", "zl")
PLANE = ("y", "x")
DEPTH = ("zl", "clip")
ANY = pl.BlockSpec(memory_space=pl.ANY)
VMEM = pl.BlockSpec(memory_space=pltpu.VMEM)
PARAMS = pltpu.CompilerParams(vmem_limit_bytes=12 * 1024 * 1024)


def a2a(x, axes):
    return lax.all_to_all(x, axes, split_axis=0, concat_axis=0, tiled=True)


def group_size(axes):
    size = 1
    for axis in axes:
        size *= lax.axis_size(axis)
    return size


def call(kernel, name, out_shape, in_specs, out_specs, *args, **more):
    return pl.pallas_call(
        kernel,
        out_shape=out_shape,
        in_specs=in_specs,
        out_specs=out_specs,
        compiler_params=PARAMS,
        name=name,
        **more,
    )(*args)


def own_kernel(
    mask_ref, video_ref, weight_ref, qkv_ref, cot_ref, own_ref, pair_ref, value_ref
):
    channels = video_ref.shape[-1]
    pair_ref[...] = lax.dot_general(
        qkv_ref[:, :channels],
        qkv_ref[:, channels : 2 * channels],
        (((1,), (1,)), ((), ())),
        preferred_element_type=F32,
    ).astype(BF)
    value_ref[...] = qkv_ref[:, 2 * channels :]

    def dot(rows, tap):
        return jnp.dot(rows, weight_ref[tap], preferred_element_type=F32)

    rows = (own_ref.shape[0] * own_ref.shape[2], own_ref.shape[3])
    v0, v1 = video_ref[:, 0].reshape(rows), video_ref[:, 1].reshape(rows)
    own_ref[:, 0] = (v0.astype(F32) + dot(v0, 0)).reshape(own_ref[:, 0].shape)
    own_ref[:, 1] = (v1.astype(F32) + (dot(v1, 0) + dot(v0, 1))).reshape(own_ref[:, 0].shape)


def early_kernel(own_ref, early_ref, weight_ref, out_ref):
    shape = (early_ref.shape[0],) + early_ref.shape[2:]
    rows = (shape[0] * shape[1], shape[2])

    def dot(rows, tap):
        return jnp.dot(rows, weight_ref[tap], preferred_element_type=F32)

    e0, e1 = early_ref[:, 0].reshape(rows), early_ref[:, 1].reshape(rows)
    h0 = own_ref[:, 0].reshape(rows) + (dot(e1, 1) + dot(e0, 2))
    h1 = own_ref[:, 1].reshape(rows) + dot(e1, 2)
    out_ref[:, 0] = h0.astype(BF).reshape(shape)
    out_ref[:, 1] = h1.astype(BF).reshape(shape)


def attend_kernel(
    hidden_ref, gain_ref, pair_ref, value_ref, att_ref, q_s, k_s, v_s
):
    pixels, channels = att_ref.shape
    step = 256
    steps = pixels // step

    def chunk(i):
        return pl.ds(i * step, step)

    def normed(i):
        wide = hidden_ref[chunk(i), :].astype(F32)
        mean = jnp.mean(wide * wide, axis=-1, keepdims=True)
        return (wide * lax.rsqrt(mean + 1e-06) * gain_ref[...]).astype(BF)

    ready = normed(0)
    for i in range(steps):
        following = normed(i + 1) if i + 1 < steps else None
        q_s[chunk(i), :] = jnp.dot(ready, pair_ref[...], preferred_element_type=F32).astype(BF)
        k_s[chunk(i), :] = ready
        v_s[chunk(i), :] = jnp.dot(ready, value_ref[...], preferred_element_type=F32).astype(BF)
        ready = following
    scale = 1.4426950408889634 / channels**0.5

    def scored(i):
        return lax.dot_general(
            q_s[chunk(i), :], k_s[...], (((1,), (1,)), ((), ())), preferred_element_type=F32
        )

    def weighed(scores):
        top = jnp.max(scores, axis=-1, keepdims=True)
        expo = jnp.exp2((scores - top) * scale)
        return expo.astype(BF), jnp.sum(expo, axis=-1, keepdims=True)

    def attended(expo, total):
        mixed = jnp.dot(expo, v_s[...], preferred_element_type=F32)
        return (mixed * (1.0 / total)).astype(BF)

    stages = [{} for _ in range(2)]
    for t in range(steps + 2):
        if t < steps:
            stages[0][t] = scored(t)
        if 0 <= t - 1 < steps:
            stages[1][t - 1] = weighed(stages[0].pop(t - 1))
        if 0 <= t - 2 < steps:
            att_ref[chunk(t - 2), :] = attended(*stages[1].pop(t - 2))


def masked_into(live_ref, mask_ref, cot_ref):
    clips, frames, tile = cot_ref.shape[:3]
    for clip in range(clips):
        for frame in range(frames):
            at = clip * frames + frame
            live_ref[pl.ds(at * tile, tile), :] = cot_ref[clip, frame] * mask_ref[at : at + 1, :]


def half_grad(att_ref, live_ref, half, split):
    return lax.dot_general(
        att_ref[:, pl.ds(pl.multiple_of(half * split, split), split)],
        live_ref[...],
        (((0,), (0,)), ((), ())),
        preferred_element_type=F32,
    )


def own_rows(hidden_ref, att_ref, wo_ref, out_ref):
    out_ref[...] = (
        hidden_ref[...].astype(F32)
        + jnp.dot(att_ref[...], wo_ref[...], preferred_element_type=F32)
    ).astype(BF)


def before_kernel(
    mask_ref, att_ref, cot_ref, hidden_ref, wo_ref,
    other_ref, live_ref, mine_ref, out_ref,
):
    masked_into(live_ref, mask_ref, cot_ref)
    core = lax.axis_index("core")
    split = other_ref.shape[0]
    other_ref[...] = half_grad(att_ref, live_ref, 1 - core, split).astype(BF)

    @pl.when(core == 0)
    def _():
        mine_ref[...] = half_grad(att_ref, live_ref, 0, split)
        own_rows(hidden_ref, att_ref, wo_ref, out_ref)


def during_kernel(
    att_ref, live_ref, hidden_ref, wo_ref, mine_in, out_in, mine_ref, out_ref
):
    core = lax.axis_index("core")

    @pl.when(core == 1)
    def _():
        own_rows(hidden_ref, att_ref, wo_ref, out_ref)
        mine_ref[...] = half_grad(att_ref, live_ref, 1, mine_ref.shape[0])

    @pl.when(core == 0)
    def _():
        mine_ref[...] = mine_in[...]
        out_ref[...] = out_in[...]


def deliver_kernel(src_ref, out_ref, sems):
    each = src_ref.shape[0] // sems.shape[0]
    copies = [
        pltpu.make_async_copy(src_ref.at[pl.ds(i * each, each)], out_ref.at[pl.ds(i * each, each)], sems.at[i])
        for i in range(sems.shape[0])
    ]
    for copy in copies:
        copy.start()
    for copy in copies:
        copy.wait()


def exchanged(x, axis, by):
    n = lax.axis_size(axis)
    return lax.ppermute(x, axis, [(i, i ^ by) for i in range(n)])


def spread(x, axes):
    n = group_size(axes)
    return a2a(jnp.broadcast_to(x.astype(BF)[None], (n,) + x.shape), axes)


def total_sum(mine, other):
    core = lax.axis_index("core")
    x = mine + exchanged(other, "core", 1).astype(F32)
    n = group_size(PLANE)
    x = a2a(x.astype(BF).reshape(n, x.shape[0] // n, x.shape[1]), PLANE)
    x = jnp.sum(x.astype(F32), axis=0)
    x = jnp.sum(spread(x, DEPTH).astype(F32), axis=0).astype(BF)
    x = spread(x, PLANE).reshape(mine.shape)
    other = exchanged(x, "core", 1)
    first = jnp.where(core == 0, x, other)
    second = jnp.where(core == 0, other, x)
    return jnp.concatenate([first, second], 0).astype(F32)


def body(video, conv_weight, norm_gain, qkv_weight, out_weight, cotangent, lengths):
    clips, frames, tile, channels = video.shape
    peers = clips * frames
    slabs = lax.axis_size(TIME)
    onward = [(i, i + 2) for i in range(1, slabs - 2, 2)] + [(i, i) for i in range(0, slabs, 2)]
    early = lax.ppermute(video, TIME, onward)
    video = exchanged(video, "core", 1)
    cotangent = exchanged(cotangent, "core", 1)
    core = lax.axis_index("core")
    slab = lax.axis_index(TIME) + 1 - 2 * core
    moments = slab * frames + jnp.arange(frames, dtype=jnp.int32)
    mask = (moments[None, :] < lengths[:, None]).astype(BF).reshape(peers, 1)
    mask = jnp.broadcast_to(mask, (peers, channels))
    own, pair, value = call(
        own_kernel,
        "own",
        (jax.ShapeDtypeStruct(video.shape, F32),) + (jax.ShapeDtypeStruct(out_weight.shape, BF),) * 2,
        [VMEM] * 4 + [ANY],
        (VMEM,) * 3,
        mask, video, conv_weight, qkv_weight, cotangent,
    )
    hidden = call(
        early_kernel,
        "early",
        jax.ShapeDtypeStruct(video.shape, BF),
        [VMEM] * 3,
        VMEM,
        own, early, conv_weight,
    )
    rows = jax.ShapeDtypeStruct((peers * tile, channels), BF)
    frame = a2a(hidden.reshape(peers, tile, channels), TILE).reshape(rows.shape)
    att = call(
        attend_kernel,
        "attend",
        rows,
        [VMEM] * 4,
        VMEM,
        frame, norm_gain.reshape(1, channels), pair, value,
        scratch_shapes=[pltpu.VMEM(rows.shape, BF)] * 3,
    )
    att = a2a(att.reshape(peers, tile, channels), TILE).reshape(rows.shape)
    kept = jax.ShapeDtypeStruct((channels // 2, channels), F32)
    flat = hidden.reshape(rows.shape)
    other, live, mine, out = call(
        before_kernel,
        "before",
        (jax.ShapeDtypeStruct(kept.shape, BF), rows, kept, rows),
        [VMEM] * 5,
        (VMEM,) * 4,
        mask, att, cotangent, flat, out_weight,
    )
    mine, out = call(
        during_kernel,
        "during",
        (kept, rows),
        [VMEM] * 6,
        (VMEM,) * 2,
        att, live, flat, out_weight, mine, out,
        input_output_aliases={4: 0, 5: 1},
        cost_estimate=pl.CostEstimate(flops=1 << 29, bytes_accessed=1 << 21, transcendentals=0),
    )
    out = call(
        deliver_kernel,
        "deliver",
        rows,
        [ANY],
        ANY,
        exchanged(out, "core", 1),
        scratch_shapes=[pltpu.SemaphoreType.DMA((peers,))],
        cost_estimate=pl.CostEstimate(flops=1 << 28, bytes_accessed=1 << 21, transcendentals=0),
    )
    return out.reshape(video.shape), total_sum(mine, other)


def solution(mesh):
    fine = Mesh(mesh.devices.reshape(4, 2, 4, 2, 4), ("y", "core", "x", "zl", "clip"))
    part = P("clip", TIME, TILE, None)
    in_specs = (part, P(), P(), P(), P(), part, P("clip"))
    return jax.shard_map(body, mesh=fine, in_specs=in_specs, out_specs=(part, P()), check_vma=False)
```

```python
import functools

import jax
import jax.numpy as jnp
from jax import lax
from jax.experimental import pallas as pl
from jax.experimental.pallas import tpu as pltpu
from jax.sharding import Mesh, PartitionSpec as P

BF, F32 = jnp.bfloat16, jnp.float32
TIME = ("y", "core")
TILE = ("x", "zl")
PLANE = ("y", "x")
DEPTH = ("zl", "clip")
ANY = pl.BlockSpec(memory_space=pl.ANY)
VMEM = pl.BlockSpec(memory_space=pltpu.VMEM)
PARAMS = pltpu.CompilerParams(vmem_limit_bytes=12 * 1024 * 1024)


def a2a(x, axes):
    return lax.all_to_all(x, axes, split_axis=0, concat_axis=0, tiled=True)


def group_size(axes):
    size = 1
    for axis in axes:
        size *= lax.axis_size(axis)
    return size


def call(kernel, name, out_shape, in_specs, out_specs, *args, **more):
    return pl.pallas_call(
        kernel,
        out_shape=out_shape,
        in_specs=in_specs,
        out_specs=out_specs,
        compiler_params=PARAMS,
        name=name,
        **more,
    )(*args)


def own_kernel(
    mask_ref, video_ref, weight_ref, qkv_ref, cot_ref, own_ref, pair_ref, value_ref
):
    channels = video_ref.shape[-1]
    pair_ref[...] = lax.dot_general(
        qkv_ref[:, :channels],
        qkv_ref[:, channels : 2 * channels],
        (((1,), (1,)), ((), ())),
        preferred_element_type=F32,
    ).astype(BF)
    value_ref[...] = qkv_ref[:, 2 * channels :]

    def dot(rows, tap):
        return jnp.dot(rows, weight_ref[tap], preferred_element_type=F32)

    rows = (own_ref.shape[0] * own_ref.shape[2], own_ref.shape[3])
    v0, v1 = video_ref[:, 0].reshape(rows), video_ref[:, 1].reshape(rows)
    own_ref[:, 0] = (v0.astype(F32) + dot(v0, 0)).reshape(own_ref[:, 0].shape)
    own_ref[:, 1] = (v1.astype(F32) + (dot(v1, 0) + dot(v0, 1))).reshape(own_ref[:, 0].shape)


def early_kernel(own_ref, early_ref, weight_ref, out_ref):
    shape = (early_ref.shape[0],) + early_ref.shape[2:]
    rows = (shape[0] * shape[1], shape[2])

    def dot(rows, tap):
        return jnp.dot(rows, weight_ref[tap], preferred_element_type=F32)

    e0, e1 = early_ref[:, 0].reshape(rows), early_ref[:, 1].reshape(rows)
    h0 = own_ref[:, 0].reshape(rows) + (dot(e1, 1) + dot(e0, 2))
    h1 = own_ref[:, 1].reshape(rows) + dot(e1, 2)
    out_ref[:, 0] = h0.astype(BF).reshape(shape)
    out_ref[:, 1] = h1.astype(BF).reshape(shape)


def attend_kernel(
    hidden_ref, gain_ref, pair_ref, value_ref, att_ref, q_s, k_s, v_s
):
    pixels, channels = att_ref.shape
    step = 256
    steps = pixels // step

    def chunk(i):
        return pl.ds(i * step, step)

    def normed(i):
        wide = hidden_ref[chunk(i), :].astype(F32)
        mean = jnp.mean(wide * wide, axis=-1, keepdims=True)
        return (wide * lax.rsqrt(mean + 1e-06) * gain_ref[...]).astype(BF)

    ready = normed(0)
    for i in range(steps):
        following = normed(i + 1) if i + 1 < steps else None
        q_s[chunk(i), :] = jnp.dot(ready, pair_ref[...], preferred_element_type=F32).astype(BF)
        k_s[chunk(i), :] = ready
        v_s[chunk(i), :] = jnp.dot(ready, value_ref[...], preferred_element_type=F32).astype(BF)
        ready = following
    scale = 1.4426950408889634 / channels**0.5

    def scored(i):
        return lax.dot_general(
            q_s[chunk(i), :], k_s[...], (((1,), (1,)), ((), ())), preferred_element_type=F32
        )

    def weighed(scores):
        top = jnp.max(scores, axis=-1, keepdims=True)
        expo = jnp.exp2((scores - top) * scale)
        return expo.astype(BF), jnp.sum(expo, axis=-1, keepdims=True)

    def attended(expo, total):
        mixed = jnp.dot(expo, v_s[...], preferred_element_type=F32)
        return (mixed * (1.0 / total)).astype(BF)

    stages = [{} for _ in range(2)]
    for t in range(steps + 2):
        if t < steps:
            stages[0][t] = scored(t)
        if 0 <= t - 1 < steps:
            stages[1][t - 1] = weighed(stages[0].pop(t - 1))
        if 0 <= t - 2 < steps:
            att_ref[chunk(t - 2), :] = attended(*stages[1].pop(t - 2))


def masked_into(live_ref, mask_ref, cot_ref):
    clips, frames, tile = cot_ref.shape[:3]
    for clip in range(clips):
        for frame in range(frames):
            at = clip * frames + frame
            live_ref[pl.ds(at * tile, tile), :] = cot_ref[clip, frame] * mask_ref[at : at + 1, :]


def half_grad(att_ref, live_ref, half, split):
    return lax.dot_general(
        att_ref[:, pl.ds(pl.multiple_of(half * split, split), split)],
        live_ref[...],
        (((0,), (0,)), ((), ())),
        preferred_element_type=F32,
    )


def own_rows(hidden_ref, att_ref, wo_ref, out_ref):
    out_ref[...] = (
        hidden_ref[...].astype(F32)
        + jnp.dot(att_ref[...], wo_ref[...], preferred_element_type=F32)
    ).astype(BF)


def before_kernel(
    mask_ref, att_ref, cot_ref, hidden_ref, wo_ref,
    other_ref, live_ref, mine_ref, out_ref,
):
    masked_into(live_ref, mask_ref, cot_ref)
    core = lax.axis_index("core")
    split = other_ref.shape[0]
    other_ref[...] = half_grad(att_ref, live_ref, 1 - core, split).astype(BF)

    @pl.when(core == 0)
    def _():
        mine_ref[...] = half_grad(att_ref, live_ref, 0, split)
        own_rows(hidden_ref, att_ref, wo_ref, out_ref)


def during_kernel(
    att_ref, live_ref, hidden_ref, wo_ref, mine_in, out_in, mine_ref, out_ref
):
    core = lax.axis_index("core")

    @pl.when(core == 1)
    def _():
        own_rows(hidden_ref, att_ref, wo_ref, out_ref)
        mine_ref[...] = half_grad(att_ref, live_ref, 1, mine_ref.shape[0])

    @pl.when(core == 0)
    def _():
        mine_ref[...] = mine_in[...]
        out_ref[...] = out_in[...]


def deliver_kernel(src_ref, half_ref, out_ref, total_ref, wide, sems, sem):
    each = src_ref.shape[0] // sems.shape[0]
    copies = [
        pltpu.make_async_copy(src_ref.at[pl.ds(i * each, each)], out_ref.at[pl.ds(i * each, each)], sems.at[i])
        for i in range(sems.shape[0])
    ]
    for copy in copies:
        copy.start()
    rows = half_ref.shape[0]
    wide[...] = half_ref[...].astype(F32)
    at = pl.ds(pl.multiple_of(lax.axis_index("core") * rows, rows), rows)
    copies.append(pltpu.make_async_copy(wide, total_ref.at[at], sem))
    copies[-1].start()
    for copy in copies:
        copy.wait()


def complete_kernel(half_ref, total_in, total_ref, wide, sem):
    rows = half_ref.shape[0]
    wide[...] = half_ref[...].astype(F32)
    at = pl.ds(pl.multiple_of((1 - lax.axis_index("core")) * rows, rows), rows)
    copy = pltpu.make_async_copy(wide, total_ref.at[at], sem)
    copy.start()
    copy.wait()


def exchanged(x, axis, by):
    n = lax.axis_size(axis)
    return lax.ppermute(x, axis, [(i, i ^ by) for i in range(n)])


def spread(x, axes):
    n = group_size(axes)
    return a2a(jnp.broadcast_to(x.astype(BF)[None], (n,) + x.shape), axes)


def total_sum(mine, other):
    x = mine + exchanged(other, "core", 1).astype(F32)
    n = group_size(PLANE)
    x = a2a(x.astype(BF).reshape(n, x.shape[0] // n, x.shape[1]), PLANE)
    x = jnp.sum(x.astype(F32), axis=0)
    x = jnp.sum(spread(x, DEPTH).astype(F32), axis=0).astype(BF)
    x = spread(x, PLANE).reshape(mine.shape)
    return x


def body(video, conv_weight, norm_gain, qkv_weight, out_weight, cotangent, lengths):
    clips, frames, tile, channels = video.shape
    peers = clips * frames
    slabs = lax.axis_size(TIME)
    onward = [(i, i + 2) for i in range(1, slabs - 2, 2)] + [(i, i) for i in range(0, slabs, 2)]
    early = lax.ppermute(video, TIME, onward)
    video = exchanged(video, "core", 1)
    cotangent = exchanged(cotangent, "core", 1)
    core = lax.axis_index("core")
    slab = lax.axis_index(TIME) + 1 - 2 * core
    moments = slab * frames + jnp.arange(frames, dtype=jnp.int32)
    mask = (moments[None, :] < lengths[:, None]).astype(BF).reshape(peers, 1)
    mask = jnp.broadcast_to(mask, (peers, channels))
    own, pair, value = call(
        own_kernel,
        "own",
        (jax.ShapeDtypeStruct(video.shape, F32),) + (jax.ShapeDtypeStruct(out_weight.shape, BF),) * 2,
        [VMEM] * 4 + [ANY],
        (VMEM,) * 3,
        mask, video, conv_weight, qkv_weight, cotangent,
    )
    hidden = call(
        early_kernel,
        "early",
        jax.ShapeDtypeStruct(video.shape, BF),
        [VMEM] * 3,
        VMEM,
        own, early, conv_weight,
    )
    rows = jax.ShapeDtypeStruct((peers * tile, channels), BF)
    frame = a2a(hidden.reshape(peers, tile, channels), TILE).reshape(rows.shape)
    att = call(
        attend_kernel,
        "attend",
        rows,
        [VMEM] * 4,
        VMEM,
        frame, norm_gain.reshape(1, channels), pair, value,
        scratch_shapes=[pltpu.VMEM(rows.shape, BF)] * 3,
    )
    att = a2a(att.reshape(peers, tile, channels), TILE).reshape(rows.shape)
    kept = jax.ShapeDtypeStruct((channels // 2, channels), F32)
    flat = hidden.reshape(rows.shape)
    other, live, mine, out = call(
        before_kernel,
        "before",
        (jax.ShapeDtypeStruct(kept.shape, BF), rows, kept, rows),
        [VMEM] * 5,
        (VMEM,) * 4,
        mask, att, cotangent, flat, out_weight,
    )
    mine, out = call(
        during_kernel,
        "during",
        (kept, rows),
        [VMEM] * 6,
        (VMEM,) * 2,
        att, live, flat, out_weight, mine, out,
        input_output_aliases={4: 0, 5: 1},
        cost_estimate=pl.CostEstimate(flops=1 << 29, bytes_accessed=1 << 21, transcendentals=0),
    )
    half = total_sum(mine, other)
    whole = jax.ShapeDtypeStruct((channels, channels), F32)
    out, total = call(
        deliver_kernel,
        "deliver",
        (rows, whole),
        [ANY, VMEM],
        (ANY, ANY),
        exchanged(out, "core", 1), half,
        scratch_shapes=[
            pltpu.VMEM(half.shape, F32),
            pltpu.SemaphoreType.DMA((peers,)),
            pltpu.SemaphoreType.DMA,
        ],
        cost_estimate=pl.CostEstimate(flops=1 << 28, bytes_accessed=1 << 21, transcendentals=0),
    )
    total = call(
        complete_kernel,
        "complete",
        whole,
        [VMEM, ANY],
        ANY,
        exchanged(half, "core", 1), total,
        input_output_aliases={1: 0},
        scratch_shapes=[pltpu.VMEM(half.shape, F32), pltpu.SemaphoreType.DMA],
    )
    return out.reshape(video.shape), total


def solution(mesh):
    fine = Mesh(mesh.devices.reshape(4, 2, 4, 2, 4), ("y", "core", "x", "zl", "clip"))
    part = P("clip", TIME, TILE, None)
    in_specs = (part, P(), P(), P(), P(), part, P("clip"))
    return jax.shard_map(body, mesh=fine, in_specs=in_specs, out_specs=(part, P()), check_vma=False)
```
